32 devices in a mesh: rows: 32 (over z, y, x, core), rhs: 1.
Axes of the slice: x: 2, y: 2, z: 4, core: 2. Of those that a mesh axis runs over, the one named last changes fastest.
Arguments:
- rhs_block: bfloat16 [4, 32, 64, 256], P(None, 'rows', 'rhs'), may hold values from -6 to 6
- diag_inv: bfloat16 [4, 32, 256, 256], P(None, 'rows'), as said below
- off_tiles: bfloat16 [3, 32, 16, 256, 256], P(None, 'rows', 'rhs'), may hold values from -0.09375 to 0.09375
- pattern: int32 [3, 32, 16], P(None, 'rows'), may hold values from 0 to 31, all different within a row
Outputs:
- forward_sol: bfloat16 [4, 32, 64, 256], P(None, 'rows', 'rhs')
- backward_sol: bfloat16 [4, 32, 64, 256], P(None, 'rows', 'rhs')
The draws below stay inside these ranges and needn't reach their ends.
Inputs may be any that keep to these rules, and one draw needn't show every extreme that they name: `pattern`: the 16 entries of one block row are distinct. `diag_inv`: every tile is lower triangular with a positive diagonal.
All inputs are finite; a program needn't handle non-finite values.
Results may differ from the reference program's by a relative error of at most 0.013.
Values may be sent and summed in bfloat16 or wider, within the bound.
No kernel may reach another device: no remote copies, remote signals or barrier semaphores. Data moves between devices by JAX's collectives and lax.ppermute only.
A program may use at most 64 MiB of HBM per device.

```python
import math
import jax
import jax.numpy as jnp
from jax import lax

B = 256
LEVELS = 4
NBL = 32
K = 16
NRHS = 64


def draw_diag_inv(key, part):
    first_key, second_key = jax.random.split(key)
    full_shape = (LEVELS, NBL, B, B)
    row_index = lax.broadcasted_iota(jnp.int32, (B, B), 0)
    col_index = lax.broadcasted_iota(jnp.int32, (B, B), 1)
    strict_mask = (row_index > col_index).astype(jnp.float32)
    identity = (row_index == col_index).astype(jnp.float32)
    strict = jax.random.normal(first_key, full_shape, jnp.float32) * (0.5 / math.sqrt(B))
    diagonal = jax.random.uniform(second_key, (LEVELS, NBL, B), jnp.float32, 0.7, 1.3)
    return (strict * strict_mask + diagonal[..., :, None] * identity).astype(jnp.bfloat16)


def steps_of(own_key, shape, shards, smallest, high):
    level = 1.0
    for position, parts in shards:
        draws = jax.random.uniform(jax.random.fold_in(jax.random.fold_in(own_key, 6), position), (parts,), jnp.float32, smallest / len(shards), high / len(shards))
        level = level * jnp.repeat(jnp.exp(draws), shape[position] // parts).reshape((-1,) + (1,) * (len(shape) - 1 - position))
    return level


def distinct(key, rows, amount, top, lift):
    order = jax.random.permutation(jax.random.fold_in(key, 1), amount)
    boost = order
    for power in range(3):
        boost = boost * boost // amount
    boost = boost * lift // amount
    tickets = jax.random.randint(jax.random.fold_in(key, 2), (rows, amount), 0, 4096) + boost
    holders = jax.random.permutation(jax.random.fold_in(key, 3), rows)[jnp.arange(amount) % rows]
    tickets = jnp.where(jnp.arange(rows)[:, None] == holders[None, :], 1 << 14, tickets)
    priority = tickets * amount + jnp.arange(amount)
    return lax.top_k(priority.astype(jnp.int32), top)[1].astype(jnp.int32)


def bell_draw(stream_key, shape, scale, reach, cuts=(), kind=jnp.bfloat16):
    values = jax.random.normal(stream_key, shape, jnp.float32) * scale
    if len(cuts) > 0:
        values = steps_of(stream_key, shape, cuts, -0.22, 0.18) * values
    return jnp.clip(values, min=-reach, max=reach).astype(kind)


def setup_inputs(seed: int = 0) -> dict:
    seeds = jax.random.split(jax.random.key(seed), 5)
    rhs_block = bell_draw(seeds[0], (LEVELS, NBL, NRHS, B), 1.0, 6.0, ((1, 32),))
    diag_inv = draw_diag_inv(jax.random.fold_in(seeds[4], 71), 0)
    off_tiles = bell_draw(seeds[2], (LEVELS - 1, NBL, K, B, B), (K * B) ** -0.5, 0.09375, ((1, 32),))
    pattern = distinct(seeds[3], (LEVELS - 1) * NBL, NBL, K, 4096).reshape((LEVELS - 1, NBL, K))
    return {"rhs_block": rhs_block, "diag_inv": diag_inv, "off_tiles": off_tiles, "pattern": pattern}


def reference(rhs_block, diag_inv, off_tiles, pattern):
    inverses = diag_inv.astype(jnp.float32)
    forward = [jnp.einsum("nrc,nac->nra", rhs_block[0].astype(jnp.float32), inverses[0]).astype(jnp.bfloat16)]
    for level_now in range(1, LEVELS):
        previous = forward[-1]

        def couple_row(operands):
            couplings, targets = operands
            picked = jnp.take(previous, targets.astype(jnp.int32), axis=0).astype(jnp.float32)
            return jnp.einsum("krc,kac->ra", picked, couplings.astype(jnp.float32))

        coupled = lax.map(couple_row, (off_tiles[level_now - 1], pattern[level_now - 1]))
        residual = (rhs_block[level_now].astype(jnp.float32) - coupled).astype(jnp.bfloat16)
        forward.append(jnp.einsum("nrc,nac->nra", residual.astype(jnp.float32), inverses[level_now]).astype(jnp.bfloat16))
    backward = [None] * LEVELS
    backward[LEVELS - 1] = jnp.einsum("nra,nac->nrc", forward[-1].astype(jnp.float32), inverses[LEVELS - 1]).astype(jnp.bfloat16)
    for level_now in range(LEVELS - 2, -1, -1):
        def push_row(pushed, operands):
            couplings, targets, values = operands
            products = jnp.einsum("ra,kac->krc", values.astype(jnp.float32), couplings.astype(jnp.float32))
            return pushed.at[targets.astype(jnp.int32)].add(products), None

        initial = jnp.zeros((NBL, NRHS, B), jnp.float32)
        pushed = lax.scan(push_row, initial, (off_tiles[level_now], pattern[level_now], backward[level_now + 1]))[0]
        residual = (forward[level_now].astype(jnp.float32) - pushed).astype(jnp.bfloat16)
        backward[level_now] = jnp.einsum("nra,nac->nrc", residual.astype(jnp.float32), inverses[level_now]).astype(jnp.bfloat16)
    return jnp.stack(forward), jnp.stack(backward)
```

```python
import functools

import jax
import jax.numpy as jnp
from jax import lax
from jax.experimental import pallas as pl
from jax.experimental.pallas import tpu as pltpu
from jax.sharding import PartitionSpec as P

VMEM_SPEC = pl.BlockSpec(memory_space=pltpu.VMEM)
SMEM_SPEC = pl.BlockSpec(memory_space=pltpu.SMEM)
VMEM_GRANT = 24 * 1024 * 1024


def swap(value, mask):
    size = lax.axis_size("rows")
    return lax.ppermute(value, "rows", [(i, i ^ mask) for i in range(size)])


def times_transposed(left, right):
    return lax.dot_general(left, right, (((1,), (1,)), ((), ())), preferred_element_type=jnp.float32)


def times(left, right):
    return jnp.dot(left, right, preferred_element_type=jnp.float32)


def call(kernel, out_shape, operands, smem=0, scratch=(), flops=0, moved=0):
    return pl.pallas_call(
        kernel,
        out_shape=out_shape,
        in_specs=[SMEM_SPEC] * smem + [VMEM_SPEC] * (len(operands) - smem),
        out_specs=jax.tree.map(lambda _: VMEM_SPEC, out_shape),
        scratch_shapes=list(scratch),
        compiler_params=pltpu.CompilerParams(vmem_limit_bytes=VMEM_GRANT),
        cost_estimate=pl.CostEstimate(flops=flops, bytes_accessed=moved, transcendentals=0),
    )(*operands)


def first_kernel(rhs_own, rhs_other, diag_own, diag_other, out):
    out[0] = times_transposed(rhs_own[...], diag_own[...]).astype(out.dtype)
    out[1] = times_transposed(rhs_other[...], diag_other[...]).astype(out.dtype)


def gather_columns(parts, held):
    count = parts[0].shape[0] * 2
    for j, part in enumerate(parts):
        for z in range(part.shape[0]):
            for s in range(2):
                held[j * count + z * 2 + s] = part[z, s]


def forward_step(slots, parts, tiles, rhs, diag, held):
    gather_columns(parts, held)
    solved = []
    for i in range(2):
        total = None
        for k in range(tiles[i].shape[0]):
            term = times_transposed(held[slots[i, k]], tiles[i][k])
            total = term if total is None else total + term
        residual = (rhs[i][...].astype(jnp.float32) - total).astype(jnp.bfloat16)
        solved.append(times_transposed(residual, diag[i][...]).astype(jnp.bfloat16))
    return solved


def push_step(slots, solved, tiles, total):
    total[...] = jnp.zeros_like(total)
    for i in range(2):
        for k in range(tiles[i].shape[0]):
            total[slots[i, k]] += times(solved[i], tiles[i][k])


def spread(total, keep, outs):
    count = keep.shape[0] * 2
    for z in range(keep.shape[0]):
        for s in range(2):
            keep[z, s] = total[z * 2 + s]
            for j, out in enumerate(outs):
                out[z, s] = total[(j + 1) * count + z * 2 + s].astype(out.dtype)


def forward_kernel(slots, *refs):
    parts, (t0, t1, r0, r1, d0, d1, out, held) = refs[:-8], refs[-8:]
    solved = forward_step(slots, parts, (t0, t1), (r0, r1), (d0, d1), held)
    out[0], out[1] = solved


def turn_kernel(slots, push_slots, *refs):
    parts = refs[:4]
    t0, t1, r0, r1, d0, d1, p0, p1, out, back, keep, o1, o2, o3, held, total = refs[4:]
    solved = forward_step(slots, parts, (t0, t1), (r0, r1), (d0, d1), held)
    out[0], out[1] = solved
    down = [times(solved[i], d[...]).astype(jnp.bfloat16) for i, d in enumerate((d0, d1))]
    back[0], back[1] = down
    push_step(push_slots, down, (p0, p1), total)
    spread(total, keep, (o1, o2, o3))


def reduce_kernel(keep, a, b, c, own, *outs):
    for z in range(keep.shape[0]):
        terms = [part[z].astype(jnp.float32) for part in (a, b, c)]
        value = keep[z] + ((terms[0] + terms[1]) + terms[2])
        if z == 0:
            own[...] = value
        else:
            outs[z - 1][...] = value.astype(jnp.bfloat16)


def backward_step(own, arrived, known, diag):
    pushed = own[...]
    for part in arrived:
        pushed = pushed + part[...].astype(jnp.float32)
    residual = (known[...].astype(jnp.float32) - pushed).astype(jnp.bfloat16)
    return [times(residual[i], d[...]).astype(jnp.bfloat16) for i, d in enumerate(diag)]


def backward_kernel(push_slots, own, known, d0, d1, p0, p1, *refs):
    arrived, (back, keep, o1, o2, o3, total) = refs[:-6], refs[-6:]
    down = backward_step(own, arrived, known, (d0, d1))
    back[0], back[1] = down
    push_step(push_slots, down, (p0, p1), total)
    spread(total, keep, (o1, o2, o3))


def last_kernel(own, known, d0, d1, *refs):
    arrived, back = refs[:-1], refs[-1]
    down = backward_step(own, arrived, known, (d0, d1))
    back[0], back[1] = down


def join_kernel(core, own, other, out):
    half = own.shape[1]
    here = pl.multiple_of(core[0] * half, half)
    there = pl.multiple_of((1 - core[0]) * half, half)
    out[:, 0, pl.ds(here, half)] = own[...]
    out[:, 0, pl.ds(there, half)] = other[...]


def body(rhs_block, diag_inv, off_tiles, pattern):
    levels, _, width, size = rhs_block.shape
    devices = lax.axis_size("rows")
    half = width // 2
    me = lax.axis_index("rows")
    core = lax.rem(me, 2)
    low = [2 * j for j in range(4)]
    high = [8 * j for j in range(devices // 8)]
    deep = len(high)
    if lax.axis_size("rhs") > 1:
        off_tiles = lax.all_gather(off_tiles, "rhs", axis=2, tiled=True)
    fan = off_tiles.shape[2]

    rhs = rhs_block[:, 0]
    rhs_own = lax.dynamic_slice_in_dim(rhs, core * half, half, 1)
    rhs_other = swap(lax.dynamic_slice_in_dim(rhs, (1 - core) * half, half, 1), 1)
    diag_own = [diag_inv[l, 0] for l in range(levels)]
    diag_other = [swap(d, 1) for d in diag_own]
    both = jnp.stack([pattern[:, 0], swap(pattern[:, 0], 1)], axis=1)
    place = jnp.bitwise_xor(both, me.astype(jnp.int32))
    slots = ((place >> 1) & 3) * (2 * deep) + (place >> 3) * 2 + (place & 1)
    tiles_own = [off_tiles[l, 0] for l in range(levels - 1)]
    tiles_other = [swap(t, 1) for t in tiles_own]

    pair = jax.ShapeDtypeStruct((2, half, size), jnp.bfloat16)
    pair_wide = jax.ShapeDtypeStruct((2, half, size), jnp.float32)
    column = jax.ShapeDtypeStruct((deep, 2, half, size), jnp.bfloat16)
    column_wide = jax.ShapeDtypeStruct((deep, 2, half, size), jnp.float32)
    held = pltpu.VMEM((devices, half, size), jnp.bfloat16)
    total = pltpu.VMEM((devices, half, size), jnp.float32)
    work = 2 * 2 * fan * half * size * size

    def gathered(block):
        stack = jnp.stack([block] + [swap(block, m) for m in high[1:]])
        return [stack] + [swap(stack, m) for m in low[1:]]

    def scattered(keep, outs):
        arrived = [swap(out, m) for out, m in zip(outs, low[1:])]
        summed = call(reduce_kernel, [pair_wide] + [pair] * (deep - 1), [keep] + arrived)
        return summed[0], [swap(part, m) for part, m in zip(summed[1:], high[1:])]

    forward = [call(first_kernel, pair, [rhs_own[0], rhs_other[0], diag_own[0], diag_other[0]])]
    for l in range(1, levels - 1):
        parts = gathered(forward[-1])
        forward.append(
            call(
                forward_kernel,
                pair,
                [slots[l - 1]] + parts
                + [tiles_own[l - 1], tiles_other[l - 1], rhs_own[l], rhs_other[l], diag_own[l], diag_other[l]],
                smem=1,
                scratch=[held],
                flops=work,
            )
        )
    l = levels - 1
    parts = gathered(forward[-1])
    top, down, keep, *outs = call(
        turn_kernel,
        [pair, pair, column_wide] + [column] * 3,
        [slots[l - 1], slots[l - 1]] + parts
        + [tiles_own[l - 1], tiles_other[l - 1], rhs_own[l], rhs_other[l], diag_own[l], diag_other[l]]
        + [tiles_own[l - 1], tiles_other[l - 1]],
        smem=2,
        scratch=[held, total],
        flops=2 * work,
    )
    forward.append(top)
    backward = [None] * levels
    backward[l] = down
    for l in range(levels - 2, 0, -1):
        own, arrived = scattered(keep, outs)
        down, keep, *outs = call(
            backward_kernel,
            [pair, column_wide] + [column] * 3,
            [slots[l - 1], own, forward[l], diag_own[l], diag_other[l], tiles_own[l - 1], tiles_other[l - 1]] + arrived,
            smem=1,
            scratch=[total],
            flops=work,
        )
        backward[l] = down
    own, arrived = scattered(keep, outs)
    backward[0] = call(last_kernel, pair, [own, forward[0], diag_own[0], diag_other[0]] + arrived)

    where = core.astype(jnp.int32)[None]
    whole = jax.ShapeDtypeStruct((levels, 1, width, size), jnp.bfloat16)

    def joined(blocks):
        mine = jnp.stack([b[0] for b in blocks])
        other = swap(jnp.stack([b[1] for b in blocks]), 1)
        return call(join_kernel, whole, [where, mine, other], smem=1)

    return joined(forward), joined(backward)


def solution(mesh):
    return jax.shard_map(
        body,
        mesh=mesh,
        in_specs=(
            P(None, "rows", "rhs", None),
            P(None, "rows", None, None),
            P(None, "rows", "rhs", None, None),
            P(None, "rows", None),
        ),
        out_specs=(P(None, "rows", "rhs", None), P(None, "rows", "rhs", None)),
        check_vma=False,
    )
```

```python
import functools

import jax
import jax.numpy as jnp
from jax import lax
from jax.experimental import pallas as pl
from jax.experimental.pallas import tpu as pltpu
from jax.sharding import PartitionSpec as P

VMEM_SPEC = pl.BlockSpec(memory_space=pltpu.VMEM)
SMEM_SPEC = pl.BlockSpec(memory_space=pltpu.SMEM)
ANY_SPEC = pl.BlockSpec(memory_space=pl.ANY)
HBM_SPEC = pl.BlockSpec(memory_space=pltpu.HBM)
VMEM_GRANT = 8 * 1024 * 1024
PLANE = (6, 2, 4)


def swap(value, mask):
    size = lax.axis_size("rows")
    return lax.ppermute(value, "rows", [(i, i ^ mask) for i in range(size)])


def times_transposed(left, right):
    return lax.dot_general(left, right, (((1,), (1,)), ((), ())), preferred_element_type=jnp.float32)


def times(left, right):
    return jnp.dot(left, right, preferred_element_type=jnp.float32)


def call(kernel, out_shape, operands, in_specs=None, scratch=(), flops=0):
    return pl.pallas_call(
        kernel,
        out_shape=out_shape,
        in_specs=[VMEM_SPEC] * len(operands) if in_specs is None else in_specs,
        out_specs=jax.tree.map(lambda _: VMEM_SPEC, out_shape),
        scratch_shapes=list(scratch),
        compiler_params=pltpu.CompilerParams(vmem_limit_bytes=VMEM_GRANT),
        cost_estimate=pl.CostEstimate(flops=flops, bytes_accessed=0, transcendentals=0),
    )(*operands)


def side(index):
    return jnp.bitwise_and(index, 1)


def halves(width):
    mine = side(lax.axis_index("rows"))
    half = width // 2
    return (
        pl.ds(pl.multiple_of(mine * half, half), half),
        pl.ds(pl.multiple_of((1 - mine) * half, half), half),
    )


def first_kernel(rhs, diag, rhs_mine, rhs_sent, mine, sent, rhs_held, diag_held, arrived):
    here, there = halves(rhs.shape[2])
    loads = [
        pltpu.make_async_copy(rhs, rhs_held, arrived.at[0]),
        pltpu.make_async_copy(diag.at[0, 0], diag_held, arrived.at[1]),
    ]
    for load in loads:
        load.start()
    for load in loads:
        load.wait()
    sent[...] = times_transposed(rhs_held[0, 0, there], diag_held[...]).astype(sent.dtype)
    mine[...] = times_transposed(rhs_held[0, 0, here], diag_held[...]).astype(mine.dtype)
    for l in range(rhs.shape[0]):
        rhs_mine[l] = rhs_held[l, 0, here]
        rhs_sent[l] = rhs_held[l, 0, there]


def place_kernel(
    level, solve_levels, own_pattern, other_pattern, after, tiles0, tiles1, diag0, diag1, spread, diag, held, arrived
):
    me = lax.axis_index("rows")
    deep = spread.shape[1] // 8
    loads = []
    for i, (tiles, inverse) in enumerate(((tiles0, diag0), (tiles1, diag1))):
        loads.append(pltpu.make_async_copy(tiles.at[level - 1, 0], held.at[i], arrived.at[i]))
        for n, l in enumerate(solve_levels):
            loads.append(pltpu.make_async_copy(inverse.at[l, 0], diag.at[n, i], arrived.at[2 + 2 * n + i]))
    for load in loads:
        load.start()

    def clear(e, nothing):
        for i in range(2):
            spread[i, e] = jnp.zeros(spread.shape[2:], spread.dtype)
        return nothing

    lax.fori_loop(0, spread.shape[1], clear, 0)
    for load in loads:
        load.wait()
    for i, pattern in enumerate((own_pattern, other_pattern)):
        for k in range(held.shape[1]):
            away = jnp.bitwise_xor(pattern[level - 1, 0, k], me)
            flat = jnp.bitwise_and(away, 6)
            part = jnp.where(flat == PLANE[0], 1, jnp.where(flat == PLANE[1], 2, jnp.where(flat == PLANE[2], 3, 0)))
            spread[i, part * (2 * deep) + (away >> 3) * 2 + side(away)] = held[i, k]


def own_kernel(spread, stack, out):
    for i in range(2):
        out[i] = meet(stack, spread, i, 0, None)


def meet(part, spread, i, j, total):
    deep = part.shape[0]
    for z in range(deep):
        for s in range(2):
            term = times_transposed(part[z, s], spread[i, j * 2 * deep + 2 * z + s])
            total = term if total is None else total + term
    return total


def more_kernel(j, spread, part, partial, out):
    for i in range(2):
        out[i] = meet(part, spread, i, j, partial[i])


def finish(spread, c, partial, rhs, diag):
    solved = []
    for i in range(2):
        coupled = meet(c, spread, i, 3, partial[i])
        residual = (rhs[i].astype(jnp.float32) - coupled).astype(jnp.bfloat16)
        solved.append(times_transposed(residual, diag[i]).astype(jnp.bfloat16))
    return solved


def push(solved, spread, j, out):
    deep = out.shape[0]
    for z in range(deep):
        for s in range(2):
            e = j * 2 * deep + 2 * z + s
            total = times(solved[0], spread[0, e]) + times(solved[1], spread[1, e])
            out[z, s] = total.astype(out.dtype)


def forward_kernel(level, spread, c, partial, r0, r1, diag, out):
    out[0], out[1] = finish(spread, c, partial, (r0[level], r1[level]), diag)


def turn_kernel(level, spread, c, partial, r0, r1, diag, out, back, o1, o2, o3):
    solved = finish(spread, c, partial, (r0[level], r1[level]), diag)
    out[0], out[1] = solved
    down = [times(solved[i], diag[i]).astype(jnp.bfloat16) for i in range(2)]
    back[0], back[1] = down
    for j, part in enumerate((o1, o2, o3)):
        push(down, spread, j + 1, part)


def keep_kernel(spread, back, keep):
    push((back[0], back[1]), spread, 0, keep)


def reduce_kernel(keep, a, b, c, own, *outs):
    for z in range(keep.shape[0]):
        terms = [part[z].astype(jnp.float32) for part in (a, b, c)]
        value = keep[z] + ((terms[0] + terms[1]) + terms[2])
        if z == 0:
            own[...] = value
        else:
            outs[z - 1][...] = value.astype(jnp.bfloat16)


def backward_step(own, arrived, known, diag):
    pushed = own[...]
    for part in arrived:
        pushed = pushed + part[...].astype(jnp.float32)
    residual = (known[...].astype(jnp.float32) - pushed).astype(jnp.bfloat16)
    return [times(residual[i], diag[i]).astype(jnp.bfloat16) for i in range(2)]


def backward_kernel(spread, own, known, diag, *refs):
    arrived, (back, o1, o2, o3) = refs[:-4], refs[-4:]
    down = backward_step(own, arrived, known, diag)
    back[0], back[1] = down
    for j, part in enumerate((o1, o2, o3)):
        push(down, spread, j + 1, part)


def last_kernel(own, known, diag, *refs):
    arrived, (mine, sent) = refs[:-2], refs[-2:]
    mine[...], sent[...] = backward_step(own, arrived, known, diag)


def split_kernel(*refs):
    blocks, (mine, sent) = refs[:-2], refs[-2:]
    for l, block in enumerate(blocks):
        mine[l] = block[0]
        sent[l] = block[1]


def join_kernel(*refs):
    pairs, out = refs[:-1], refs[-1]
    here, there = halves(out.shape[2])
    l = 0
    for mine, other in zip(pairs[0::2], pairs[1::2]):
        for m in range(mine.shape[0]):
            out[l, 0, here] = mine[m]
            out[l, 0, there] = other[m]
            l += 1


def body(rhs_block, diag_inv, off_tiles, pattern):
    levels, _, width, size = rhs_block.shape
    devices = lax.axis_size("rows")
    half = width // 2
    line = [8 * j for j in range(1, devices // 8)]
    deep = len(line) + 1
    if lax.axis_size("rhs") > 1:
        off_tiles = lax.all_gather(off_tiles, "rhs", axis=2, tiled=True)

    def shape(*dims, dtype=jnp.bfloat16):
        return jax.ShapeDtypeStruct(dims + (half, size), dtype)

    def in_hbm(value):
        return pltpu.with_memory_space_constraint(value, pltpu.HBM)

    rhs_own, rhs_sent, mine, sent = call(
        first_kernel,
        [shape(levels)] * 2 + [shape()] * 2,
        [in_hbm(rhs_block), in_hbm(diag_inv)],
        [HBM_SPEC] * 2,
        scratch=[
            pltpu.VMEM(rhs_block.shape, jnp.bfloat16),
            pltpu.VMEM((size, size), jnp.bfloat16),
            pltpu.SemaphoreType.DMA((2,)),
        ],
    )
    other_pattern = swap(pattern, 1)
    other = swap(sent, 1)
    forward = [jnp.stack([mine, other])]
    rhs_sent, diag_own, own_tiles, other, other_pattern = lax.optimization_barrier(
        (rhs_sent, diag_inv, off_tiles, other, other_pattern)
    )
    other_tiles = swap(own_tiles, 1)
    rhs_other, diag_other = swap(rhs_sent, 1), swap(diag_own, 1)
    own_tiles, diag_own = in_hbm(off_tiles), in_hbm(diag_inv)
    work = 2 * 2 * devices // 4 * half * size * size
    diag = [None] * levels

    def met(level, block):
        arrived = [block] + [swap(block, m) for m in line]
        solve_levels = (1, 0) if level == 1 else (level,)
        spread, inverses = call(
            functools.partial(place_kernel, level, solve_levels),
            [
                pltpu.VMEM((2, devices, size, size), jnp.bfloat16),
                pltpu.VMEM((len(solve_levels), 2, size, size), jnp.bfloat16),
            ],
            [pattern, other_pattern, block, own_tiles, other_tiles, diag_own, diag_other],
            [SMEM_SPEC] * 2 + [VMEM_SPEC] + [HBM_SPEC, ANY_SPEC] * 2,
            scratch=[
                pltpu.VMEM((2,) + off_tiles.shape[2:], jnp.bfloat16),
                pltpu.SemaphoreType.DMA((2 + 2 * len(solve_levels),)),
            ],
            flops=2 * work,
        )
        for n, l in enumerate(solve_levels):
            diag[l] = inverses[n]
        if level > 1:
            *arrived, spread = lax.optimization_barrier((*arrived, spread))
        stack = jnp.stack(arrived)
        parts = [swap(stack, m) for m in PLANE]
        partial = call(own_kernel, shape(2, dtype=jnp.float32), [spread, stack], flops=work)
        for j in (1, 2):
            kernel = functools.partial(more_kernel, j)
            partial = call(kernel, shape(2, dtype=jnp.float32), [spread, parts[j - 1], partial], flops=work)
        return spread, [spread, parts[2], partial, rhs_own, rhs_other, diag[level]]

    def scattered(spread, back, outs):
        keep = call(keep_kernel, shape(deep, 2, dtype=jnp.float32), [spread, back], flops=work)
        arrived = [swap(out, m) for out, m in zip(outs, PLANE)]
        summed = call(reduce_kernel, [shape(2, dtype=jnp.float32)] + [shape(2)] * (deep - 1), [keep] + arrived)
        return summed[0], [swap(part, m) for part, m in zip(summed[1:], line)]

    spreads = []
    for l in range(1, levels - 1):
        spread, operands = met(l, forward[-1])
        spreads.append(spread)
        forward.append(call(functools.partial(forward_kernel, l), shape(2), operands, flops=work))
    l = levels - 1
    spread, operands = met(l, forward[-1])
    spreads.append(spread)
    top, back, *outs = call(
        functools.partial(turn_kernel, l), [shape(2)] * 2 + [shape(deep, 2)] * 3, operands, flops=4 * work
    )
    forward.append(top)
    backward = [back]
    for l in range(levels - 2, 0, -1):
        own, arrived = scattered(spreads[l], back, outs)
        back, *outs = call(
            backward_kernel,
            [shape(2)] + [shape(deep, 2)] * 3,
            [spreads[l - 1], own, forward[l], diag[l]] + arrived,
            flops=3 * work,
        )
        backward.insert(0, back)
    own, arrived = scattered(spreads[0], back, outs)
    last, last_sent = call(last_kernel, [shape()] * 2, [own, forward[0], diag[0]] + arrived)

    whole = jax.ShapeDtypeStruct((levels, 1, width, size), jnp.bfloat16)
    mine, sent = call(split_kernel, [shape(levels)] * 2, forward)
    forward_sol = call(join_kernel, whole, [mine, swap(sent, 1)])
    mine, sent = call(split_kernel, [shape(levels - 1)] * 2, backward)
    backward_sol = call(join_kernel, whole, [last[None], swap(last_sent, 1)[None], mine, swap(sent, 1)])
    return forward_sol, backward_sol


def solution(mesh):
    return jax.shard_map(
        body,
        mesh=mesh,
        in_specs=(
            P(None, "rows", "rhs", None),
            P(None, "rows", None, None),
            P(None, "rows", "rhs", None, None),
            P(None, "rows", None),
        ),
        out_specs=(P(None, "rows", "rhs", None), P(None, "rows", "rhs", None)),
        check_vma=False,
    )
```

```python
import functools

import jax
import jax.numpy as jnp
from jax import lax
from jax.experimental import pallas as pl
from jax.experimental.pallas import tpu as pltpu
from jax.sharding import PartitionSpec as P

VMEM_SPEC = pl.BlockSpec(memory_space=pltpu.VMEM)
SMEM_SPEC = pl.BlockSpec(memory_space=pltpu.SMEM)
ANY_SPEC = pl.BlockSpec(memory_space=pl.ANY)
HBM_SPEC = pl.BlockSpec(memory_space=pltpu.HBM)
VMEM_GRANT = 8 * 1024 * 1024
PLANE = (6, 2, 4)


FIRST = 3


def swap(value, mask):
    size = lax.axis_size("rows")
    return lax.ppermute(value, "rows", [(i, i ^ mask) for i in range(size)])


def times_transposed(left, right):
    return lax.dot_general(left, right, (((1,), (1,)), ((), ())), preferred_element_type=jnp.float32)


def times(left, right):
    return jnp.dot(left, right, preferred_element_type=jnp.float32)


def call(kernel, out_shape, operands, in_specs=None, scratch=(), flops=0):
    return pl.pallas_call(
        kernel,
        out_shape=out_shape,
        in_specs=[VMEM_SPEC] * len(operands) if in_specs is None else in_specs,
        out_specs=jax.tree.map(lambda _: VMEM_SPEC, out_shape),
        scratch_shapes=list(scratch),
        compiler_params=pltpu.CompilerParams(vmem_limit_bytes=VMEM_GRANT),
        cost_estimate=pl.CostEstimate(flops=flops, bytes_accessed=0, transcendentals=0),
    )(*operands)


def side(index):
    return jnp.bitwise_and(index, 1)


def halves(width):
    mine = side(lax.axis_index("rows"))
    half = width // 2
    return (
        pl.ds(pl.multiple_of(mine * half, half), half),
        pl.ds(pl.multiple_of((1 - mine) * half, half), half),
    )


def first_kernel(rhs, diag, mine, sent, rhs_held, diag_held, arrived):
    here, there = halves(rhs.shape[2])
    loads = [
        pltpu.make_async_copy(rhs.at[0, 0], rhs_held, arrived.at[0]),
        pltpu.make_async_copy(diag.at[0, 0], diag_held, arrived.at[1]),
    ]
    for load in loads:
        load.start()
    for load in loads:
        load.wait()
    sent[...] = times_transposed(rhs_held[there], diag_held[...]).astype(sent.dtype)
    mine[...] = times_transposed(rhs_held[here], diag_held[...]).astype(mine.dtype)


def halve_kernel(after, rhs, rhs_mine, rhs_sent):
    here, there = halves(rhs.shape[2])
    for l in range(rhs.shape[0]):
        rhs_mine[l] = rhs[l, 0, here]
        rhs_sent[l] = rhs[l, 0, there]


def place_kernel(
    level, solve_levels, own_pattern, other_pattern, after, tiles0, tiles1, diag0, diag1, spread, diag, held, arrived
):
    me = lax.axis_index("rows")
    deep = spread.shape[1] // 8
    loads = []
    for i, (tiles, inverse) in enumerate(((tiles0, diag0), (tiles1, diag1))):
        loads.append(pltpu.make_async_copy(tiles.at[level - 1, 0], held.at[i], arrived.at[i]))
        for n, l in enumerate(solve_levels):
            loads.append(pltpu.make_async_copy(inverse.at[l, 0], diag.at[n, i], arrived.at[2 + 2 * n + i]))
    for load in loads:
        load.start()

    def clear(e, nothing):
        for i in range(2):
            spread[i, e] = jnp.zeros(spread.shape[2:], spread.dtype)
        return nothing

    lax.fori_loop(0, spread.shape[1], clear, 0)
    for load in loads:
        load.wait()
    for i, pattern in enumerate((own_pattern, other_pattern)):
        for k in range(held.shape[1]):
            away = jnp.bitwise_xor(pattern[level - 1, 0, k], me)
            flat = jnp.bitwise_and(away, 6)
            part = jnp.where(flat == PLANE[0], 1, jnp.where(flat == PLANE[1], 2, jnp.where(flat == PLANE[2], 3, 0)))
            spread[i, part * (2 * deep) + (away >> 3) * 2 + side(away)] = held[i, k]


def meet(part, spread, i, j):
    deep = part.shape[0]
    total = None
    for z in range(deep):
        for s in range(2):
            term = times_transposed(part[z, s], spread[i, j * 2 * deep + 2 * z + s])
            total = term if total is None else total + term
    return total


def more_kernel(j, spread, part, *refs):
    terms = [meet(part, spread, i, j) for i in range(2)]
    for i in range(2):
        refs[-1][i] = refs[0][i] + terms[i] if len(refs) > 1 else terms[i]


def finish(spread, late, partial, rhs, diag):
    terms = [None, None]
    for j, part in late:
        for i in range(2):
            term = meet(part, spread, i, j)
            terms[i] = term if terms[i] is None else terms[i] + term
    residuals = []
    for i in range(2):
        coupled = terms[i] if partial is None else partial[i] + terms[i]
        residuals.append((rhs[i].astype(jnp.float32) - coupled).astype(jnp.bfloat16))
    return [times_transposed(residuals[i], diag[i]).astype(jnp.bfloat16) for i in range(2)]


def push(solved, spread, j, out):
    deep = out.shape[0]
    for z in range(deep):
        for s in range(2):
            e = j * 2 * deep + 2 * z + s
            total = times(solved[0], spread[0, e]) + times(solved[1], spread[1, e])
            out[z, s] = total.astype(out.dtype)


def forward_kernel(level, first, spread, r0, r1, diag, *refs):
    late, partial, out = list(enumerate(refs[: 4 - first], first)), refs[4 - first] if first else None, refs[-1]
    out[0], out[1] = finish(spread, late, partial, (r0[level], r1[level]), diag)


def turn_kernel(level, first, spread, r0, r1, diag, *refs):
    late, partial, (out, back, o1, o2, o3) = list(enumerate(refs[: 4 - first], first)), refs[4 - first], refs[-5:]
    solved = finish(spread, late, partial, (r0[level], r1[level]), diag)
    out[0], out[1] = solved
    down = [times(solved[i], diag[i]).astype(jnp.bfloat16) for i in range(2)]
    back[0], back[1] = down
    for j, part in enumerate((o1, o2, o3)):
        push(down, spread, j + 1, part)


def keep_kernel(spread, back, keep):
    push((back[0], back[1]), spread, 0, keep)


def reduce_kernel(keep, a, b, c, own, *outs):
    for z in range(keep.shape[0]):
        terms = [part[z].astype(jnp.float32) for part in (a, b, c)]
        value = keep[z] + ((terms[0] + terms[1]) + terms[2])
        if z == 0:
            own[...] = value
        else:
            outs[z - 1][...] = value.astype(jnp.bfloat16)


def backward_step(own, arrived, known, diag):
    pushed = own[...]
    for part in arrived:
        pushed = pushed + part[...].astype(jnp.float32)
    residual = (known[...].astype(jnp.float32) - pushed).astype(jnp.bfloat16)
    return [times(residual[i], diag[i]).astype(jnp.bfloat16) for i in range(2)]


def backward_kernel(spread, own, known, diag, *refs):
    arrived, (back, o1, o2, o3) = refs[:-4], refs[-4:]
    down = backward_step(own, arrived, known, diag)
    back[0], back[1] = down
    for j, part in enumerate((o1, o2, o3)):
        push(down, spread, j + 1, part)


def last_kernel(own, known, diag, *refs):
    arrived, (mine, sent) = refs[:-2], refs[-2:]
    mine[...], sent[...] = backward_step(own, arrived, known, diag)


def split_kernel(*refs):
    blocks, (mine, sent) = refs[:-2], refs[-2:]
    for l, block in enumerate(blocks):
        mine[l] = block[0]
        sent[l] = block[1]


def join_kernel(*refs):
    pairs, out = refs[:-1], refs[-1]
    here, there = halves(out.shape[2])
    l = 0
    for mine, other in zip(pairs[0::2], pairs[1::2]):
        for m in range(mine.shape[0]):
            out[l, 0, here] = mine[m]
            out[l, 0, there] = other[m]
            l += 1


def body(rhs_block, diag_inv, off_tiles, pattern):
    levels, _, width, size = rhs_block.shape
    devices = lax.axis_size("rows")
    half = width // 2
    line = [8 * j for j in range(1, devices // 8)]
    deep = len(line) + 1
    if lax.axis_size("rhs") > 1:
        off_tiles = lax.all_gather(off_tiles, "rhs", axis=2, tiled=True)

    def shape(*dims, dtype=jnp.bfloat16):
        return jax.ShapeDtypeStruct(dims + (half, size), dtype)

    def in_hbm(value):
        return pltpu.with_memory_space_constraint(value, pltpu.HBM)

    own_tiles, diag_own = in_hbm(off_tiles), in_hbm(diag_inv)
    mine, sent = call(
        first_kernel,
        [shape()] * 2,
        [in_hbm(rhs_block), diag_own],
        [HBM_SPEC] * 2,
        scratch=[
            pltpu.VMEM((width, size), jnp.bfloat16),
            pltpu.VMEM((size, size), jnp.bfloat16),
            pltpu.SemaphoreType.DMA((2,)),
        ],
    )
    other_pattern = swap(pattern, 1)
    other = swap(sent, 1)
    rhs_own, rhs_sent = call(halve_kernel, [shape(levels)] * 2, [sent, rhs_block])
    rhs_sent, diag_sent, tiles_sent, other, other_pattern = lax.optimization_barrier(
        (rhs_sent, diag_inv, off_tiles, other, other_pattern)
    )
    forward = [jnp.stack([mine, other])]
    rhs_other, diag_other, other_tiles = swap(rhs_sent, 1), swap(diag_sent, 1), swap(tiles_sent, 1)
    work = 2 * 2 * devices // 4 * half * size * size
    diag = [None] * levels

    def along(block):
        return [block] + [swap(block, m) for m in line]

    def placed(level, block):
        solve_levels = (1, 0) if level == 1 else (level,)
        spread, inverses = call(
            functools.partial(place_kernel, level, solve_levels),
            [
                pltpu.VMEM((2, devices, size, size), jnp.bfloat16),
                pltpu.VMEM((len(solve_levels), 2, size, size), jnp.bfloat16),
            ],
            [in_hbm(pattern), other_pattern, block, own_tiles, other_tiles, diag_own, diag_other],
            [SMEM_SPEC] * 2 + [VMEM_SPEC] + [HBM_SPEC, ANY_SPEC] * 2,
            scratch=[
                pltpu.VMEM((2,) + off_tiles.shape[2:], jnp.bfloat16),
                pltpu.SemaphoreType.DMA((2 + 2 * len(solve_levels),)),
            ],
            flops=2 * work,
        )
        for n, l in enumerate(solve_levels):
            diag[l] = inverses[n]
        return spread

    def met(level, arrived, spread, first):
        parts = [jnp.stack(arrived)]
        parts += [swap(parts[0], m) for m in PLANE]
        partial = []
        for j in range(first):
            kernel = functools.partial(more_kernel, j)
            partial = [call(kernel, shape(2, dtype=jnp.float32), [spread, parts[j]] + partial, flops=work)]
        return [spread, rhs_own, rhs_other, diag[level]] + parts[first:] + partial

    def scattered(spread, back, outs):
        keep = call(keep_kernel, shape(deep, 2, dtype=jnp.float32), [spread, back], flops=work)
        arrived = [swap(out, m) for out, m in zip(outs, PLANE)]
        summed = call(reduce_kernel, [shape(2, dtype=jnp.float32)] + [shape(2)] * (deep - 1), [keep] + arrived)
        return summed[0], [swap(part, m) for part, m in zip(summed[1:], line)]

    arrived = along(forward[0])
    spreads = [placed(1, forward[0])]
    for l in range(1, levels - 1):
        first = FIRST
        operands = met(l, arrived, spreads[-1], first)
        forward.append(call(functools.partial(forward_kernel, l, first), shape(2), operands, flops=work))
        arrived = along(forward[l])
        spread = placed(l + 1, forward[l])
        *arrived, spread = lax.optimization_barrier((*arrived, spread))
        spreads.append(spread)
    l = levels - 1
    operands = met(l, arrived, spreads[-1], FIRST)
    top, back, *outs = call(
        functools.partial(turn_kernel, l, FIRST), [shape(2)] * 2 + [shape(deep, 2)] * 3, operands, flops=4 * work
    )
    forward.append(top)
    backward = [back]
    for l in range(levels - 2, 0, -1):
        own, arrived = scattered(spreads[l], back, outs)
        back, *outs = call(
            backward_kernel,
            [shape(2)] + [shape(deep, 2)] * 3,
            [spreads[l - 1], own, forward[l], diag[l]] + arrived,
            flops=3 * work,
        )
        backward.insert(0, back)
    own, arrived = scattered(spreads[0], back, outs)
    last, last_sent = call(last_kernel, [shape()] * 2, [own, forward[0], diag[0]] + arrived)

    whole = jax.ShapeDtypeStruct((levels, 1, width, size), jnp.bfloat16)
    mine, sent = call(split_kernel, [shape(levels)] * 2, forward)
    forward_sol = call(join_kernel, whole, [mine, swap(sent, 1)])
    mine, sent = call(split_kernel, [shape(levels - 1)] * 2, backward)
    backward_sol = call(join_kernel, whole, [last[None], swap(last_sent, 1)[None], mine, swap(sent, 1)])
    return forward_sol, backward_sol


def solution(mesh):
    return jax.shard_map(
        body,
        mesh=mesh,
        in_specs=(
            P(None, "rows", "rhs", None),
            P(None, "rows", None, None),
            P(None, "rows", "rhs", None, None),
            P(None, "rows", None),
        ),
        out_specs=(P(None, "rows", "rhs", None), P(None, "rows", "rhs", None)),
        check_vma=False,
    )
```

```python
import functools

import jax
import jax.numpy as jnp
from jax import lax
from jax.experimental import pallas as pl
from jax.experimental.pallas import tpu as pltpu
from jax.sharding import PartitionSpec as P

VMEM_SPEC = pl.BlockSpec(memory_space=pltpu.VMEM)
SMEM_SPEC = pl.BlockSpec(memory_space=pltpu.SMEM)
ANY_SPEC = pl.BlockSpec(memory_space=pl.ANY)
HBM_SPEC = pl.BlockSpec(memory_space=pltpu.HBM)
VMEM_GRANT = 8 * 1024 * 1024
PLANE = (6, 2, 4)


FIRST = 3
ROUND = 6
CROSS = (1,2,3)


def swap(value, mask):
    size = lax.axis_size("rows")
    return lax.ppermute(value, "rows", [(i, i ^ mask) for i in range(size)])


def times_transposed(left, right):
    return lax.dot_general(left, right, (((1,), (1,)), ((), ())), preferred_element_type=jnp.float32)


def times(left, right):
    return jnp.dot(left, right, preferred_element_type=jnp.float32)


def call(kernel, out_shape, operands, in_specs=None, scratch=(), flops=0):
    return pl.pallas_call(
        kernel,
        out_shape=out_shape,
        in_specs=[VMEM_SPEC] * len(operands) if in_specs is None else in_specs,
        out_specs=jax.tree.map(lambda _: VMEM_SPEC, out_shape),
        scratch_shapes=list(scratch),
        compiler_params=pltpu.CompilerParams(vmem_limit_bytes=VMEM_GRANT),
        cost_estimate=pl.CostEstimate(flops=flops, bytes_accessed=0, transcendentals=0),
    )(*operands)


def side(index):
    for bit in CROSS:
        index = index ^ ((index >> bit) & 1)
    return index & 1


def halves(width):
    mine = side(lax.axis_index("rows"))
    half = width // 2
    return (
        pl.ds(pl.multiple_of(mine * half, half), half),
        pl.ds(pl.multiple_of((1 - mine) * half, half), half),
    )


def first_kernel(rhs, diag, mine, sent, rhs_held, diag_held, arrived):
    here, there = halves(rhs.shape[2])
    loads = [
        pltpu.make_async_copy(rhs.at[0, 0], rhs_held, arrived.at[0]),
        pltpu.make_async_copy(diag.at[0, 0], diag_held, arrived.at[1]),
    ]
    for load in loads:
        load.start()
    for load in loads:
        load.wait()
    sent[...] = times_transposed(rhs_held[there], diag_held[...]).astype(sent.dtype)
    mine[...] = times_transposed(rhs_held[here], diag_held[...]).astype(mine.dtype)


def halve_kernel(after, rhs, rhs_mine, rhs_sent):
    here, there = halves(rhs.shape[2])
    for l in range(rhs.shape[0]):
        rhs_mine[l] = rhs[l, 0, here]
        rhs_sent[l] = rhs[l, 0, there]


def place_kernel(
    level, solve_levels, own_pattern, other_pattern, after, tiles0, tiles1, diag0, diag1, spread, diag, held, arrived
):
    me = lax.axis_index("rows")
    deep = spread.shape[1] // 8
    patterns, tiles = (own_pattern, other_pattern), (tiles0, tiles1)
    loads = []
    for i, inverse in enumerate((diag0, diag1)):
        for n, l in enumerate(solve_levels):
            loads.append(pltpu.make_async_copy(inverse.at[l, 0], diag.at[n, i], arrived.at[2 + 2 * n + i]))
    for load in loads:
        load.start()

    def clear():
        def clear_place(e, nothing):
            for i in range(2):
                spread[i, e] = jnp.zeros(spread.shape[2:], spread.dtype)
            return nothing

        lax.fori_loop(0, spread.shape[1], clear_place, 0)

    def place_of(i, k):
        away = jnp.bitwise_xor(patterns[i][level - 1, 0, k], me)
        flat = jnp.bitwise_and(away, 6)
        part = jnp.where(flat == PLANE[0], 1, jnp.where(flat == PLANE[1], 2, jnp.where(flat == PLANE[2], 3, 0)))
        return part * (2 * deep) + (away >> 3) * 2 + side(away)

    whole = [pltpu.make_async_copy(tiles[i].at[level - 1, 0], held.at[i], arrived.at[i]) for i in range(2)]

    def place_all():
        for load in whole:
            load.start()
        clear()
        for i in range(2):
            whole[i].wait()
            for k in range(held.shape[1]):
                spread[i, place_of(i, k)] = held[i, k]

    def place_few():
        clear()
        for i in range(2):
            for start in range(0, held.shape[1], ROUND):
                count = min(ROUND, held.shape[1] - start)
                for k in range(start, start + count):
                    tile = tiles[i].at[level - 1, 0, k]
                    pltpu.make_async_copy(tile, spread.at[i, place_of(i, k)], arrived.at[i]).start()
                some = tiles[i].at[level - 1, 0, pl.ds(start, count)]
                pltpu.make_async_copy(some, spread.at[i, pl.ds(0, count)], arrived.at[i]).wait()

    if level == 1:
        group = side(me)
        pl.when(group == 0)(place_all)
        pl.when(group == 1)(place_few)
    else:
        place_all()
    for load in loads:
        load.wait()


def meet(part, spread, i, j):
    deep = part.shape[0]
    total = None
    for z in range(deep):
        for s in range(2):
            term = times_transposed(part[z, s], spread[i, j * 2 * deep + 2 * z + s])
            total = term if total is None else total + term
    return total


def more_kernel(j, spread, part, *refs):
    terms = [meet(part, spread, i, j) for i in range(2)]
    for i in range(2):
        refs[-1][i] = refs[0][i] + terms[i] if len(refs) > 1 else terms[i]


def finish(spread, late, partial, rhs, diag):
    terms = [None, None]
    for j, part in late:
        for i in range(2):
            term = meet(part, spread, i, j)
            terms[i] = term if terms[i] is None else terms[i] + term
    residuals = []
    for i in range(2):
        coupled = terms[i] if partial is None else partial[i] + terms[i]
        residuals.append((rhs[i].astype(jnp.float32) - coupled).astype(jnp.bfloat16))
    return [times_transposed(residuals[i], diag[i]).astype(jnp.bfloat16) for i in range(2)]


def push(solved, spread, j, out):
    deep = out.shape[0]
    for z in range(deep):
        for s in range(2):
            e = j * 2 * deep + 2 * z + s
            total = times(solved[0], spread[0, e]) + times(solved[1], spread[1, e])
            out[z, s] = total.astype(out.dtype)


def forward_kernel(level, first, spread, r0, r1, diag, *refs):
    late, partial, out = list(enumerate(refs[: 4 - first], first)), refs[4 - first] if first else None, refs[-1]
    out[0], out[1] = finish(spread, late, partial, (r0[level], r1[level]), diag)


def turn_kernel(level, first, spread, r0, r1, diag, *refs):
    late, partial, (out, back, o1, o2, o3) = list(enumerate(refs[: 4 - first], first)), refs[4 - first], refs[-5:]
    solved = finish(spread, late, partial, (r0[level], r1[level]), diag)
    out[0], out[1] = solved
    down = [times(solved[i], diag[i]).astype(jnp.bfloat16) for i in range(2)]
    back[0], back[1] = down
    for j, part in enumerate((o1, o2, o3)):
        push(down, spread, j + 1, part)


def keep_kernel(spread, back, keep):
    push((back[0], back[1]), spread, 0, keep)


def reduce_kernel(keep, a, b, c, own, *outs):
    for z in range(keep.shape[0]):
        terms = [part[z].astype(jnp.float32) for part in (a, b, c)]
        value = keep[z] + ((terms[0] + terms[1]) + terms[2])
        if z == 0:
            own[...] = value
        else:
            outs[z - 1][...] = value.astype(jnp.bfloat16)


def backward_step(own, arrived, known, diag):
    pushed = own[...]
    for part in arrived:
        pushed = pushed + part[...].astype(jnp.float32)
    residual = (known[...].astype(jnp.float32) - pushed).astype(jnp.bfloat16)
    return [times(residual[i], diag[i]).astype(jnp.bfloat16) for i in range(2)]


def backward_kernel(spread, own, known, diag, *refs):
    arrived, (back, o1, o2, o3) = refs[:-4], refs[-4:]
    down = backward_step(own, arrived, known, diag)
    back[0], back[1] = down
    for j, part in enumerate((o1, o2, o3)):
        push(down, spread, j + 1, part)


def last_kernel(levels, own, known, diag, *refs):
    split = len(refs) - 2 - (2 * levels - 1)
    arrived, blocks, (mine, sent) = refs[:split], refs[split:-2], refs[-2:]
    solved = backward_step(own, arrived, known, diag)
    for n, block in enumerate(blocks):
        n += n >= levels
        mine[n] = block[0]
        sent[n] = block[1]
    mine[levels], sent[levels] = solved


def join_kernel(mine, other, *outs):
    here, there = halves(outs[0].shape[2])
    levels = outs[0].shape[0]
    for n, out in enumerate(outs):
        for l in range(levels):
            out[l, 0, here] = mine[n * levels + l]
            out[l, 0, there] = other[n * levels + l]


def body(rhs_block, diag_inv, off_tiles, pattern):
    levels, _, width, size = rhs_block.shape
    devices = lax.axis_size("rows")
    half = width // 2
    line = [8 * j + side(8 * j) for j in range(1, devices // 8)]
    plane = [m + side(m) for m in PLANE]
    deep = len(line) + 1
    if lax.axis_size("rhs") > 1:
        off_tiles = lax.all_gather(off_tiles, "rhs", axis=2, tiled=True)

    def shape(*dims, dtype=jnp.bfloat16):
        return jax.ShapeDtypeStruct(dims + (half, size), dtype)

    def in_hbm(value):
        return pltpu.with_memory_space_constraint(value, pltpu.HBM)

    own_tiles, diag_own = in_hbm(off_tiles), in_hbm(diag_inv)
    mine, sent = call(
        first_kernel,
        [shape()] * 2,
        [in_hbm(rhs_block), diag_own],
        [HBM_SPEC] * 2,
        scratch=[
            pltpu.VMEM((width, size), jnp.bfloat16),
            pltpu.VMEM((size, size), jnp.bfloat16),
            pltpu.SemaphoreType.DMA((2,)),
        ],
    )
    other_pattern = swap(pattern, 1)
    other = swap(sent, 1)
    rhs_own, rhs_sent = call(halve_kernel, [shape(levels)] * 2, [sent, rhs_block])
    rhs_sent, diag_sent, tiles_sent, other, other_pattern = lax.optimization_barrier(
        (rhs_sent, diag_inv, off_tiles, other, other_pattern)
    )
    forward = [jnp.stack([mine, other])]
    rhs_other, diag_other, other_tiles = swap(rhs_sent, 1), swap(diag_sent, 1), swap(tiles_sent, 1)
    work = 2 * 2 * devices // 4 * half * size * size
    diag = [None] * levels

    def along(block):
        return [block] + [swap(block, m) for m in line]

    def placed(level, block):
        solve_levels = (1, 0) if level == 1 else (level,)
        spread, inverses = call(
            functools.partial(place_kernel, level, solve_levels),
            [
                pltpu.VMEM((2, devices, size, size), jnp.bfloat16),
                pltpu.VMEM((len(solve_levels), 2, size, size), jnp.bfloat16),
            ],
            [in_hbm(pattern), other_pattern, block, own_tiles, other_tiles, diag_own, diag_other],
            [SMEM_SPEC] * 2 + [VMEM_SPEC] + [HBM_SPEC, ANY_SPEC] * 2,
            scratch=[
                pltpu.VMEM((2,) + off_tiles.shape[2:], jnp.bfloat16),
                pltpu.SemaphoreType.DMA((2 + 2 * len(solve_levels),)),
            ],
            flops=2 * work,
        )
        for n, l in enumerate(solve_levels):
            diag[l] = inverses[n]
        return spread

    def met(level, arrived, spread, first):
        parts = [jnp.stack(arrived)]
        parts += [swap(parts[0], m) for m in plane]
        partial = []
        for j in range(first):
            kernel = functools.partial(more_kernel, j)
            partial = [call(kernel, shape(2, dtype=jnp.float32), [spread, parts[j]] + partial, flops=work)]
        return [spread, rhs_own, rhs_other, diag[level]] + parts[first:] + partial

    def scattered(spread, back, outs):
        keep = call(keep_kernel, shape(deep, 2, dtype=jnp.float32), [spread, back], flops=work)
        arrived = [swap(out, m) for out, m in zip(outs, plane)]
        summed = call(reduce_kernel, [shape(2, dtype=jnp.float32)] + [shape(2)] * (deep - 1), [keep] + arrived)
        return summed[0], [swap(part, m) for part, m in zip(summed[1:], line)]

    arrived = along(forward[0])
    spreads = [placed(1, forward[0])]
    for l in range(1, levels - 1):
        first = FIRST
        operands = met(l, arrived, spreads[-1], first)
        forward.append(call(functools.partial(forward_kernel, l, first), shape(2), operands, flops=work))
        arrived = along(forward[l])
        spread = placed(l + 1, forward[l])
        *arrived, spread = lax.optimization_barrier((*arrived, spread))
        spreads.append(spread)
    l = levels - 1
    operands = met(l, arrived, spreads[-1], FIRST)
    top, back, *outs = call(
        functools.partial(turn_kernel, l, FIRST), [shape(2)] * 2 + [shape(deep, 2)] * 3, operands, flops=4 * work
    )
    forward.append(top)
    backward = [back]
    for l in range(levels - 2, 0, -1):
        own, arrived = scattered(spreads[l], back, outs)
        back, *outs = call(
            backward_kernel,
            [shape(2)] + [shape(deep, 2)] * 3,
            [spreads[l - 1], own, forward[l], diag[l]] + arrived,
            flops=3 * work,
        )
        backward.insert(0, back)
    own, arrived = scattered(spreads[0], back, outs)
    mine, sent = call(
        functools.partial(last_kernel, levels),
        [shape(2 * levels)] * 2,
        [own, forward[0], diag[0]] + arrived + forward + backward,
    )
    whole = jax.ShapeDtypeStruct((levels, 1, width, size), jnp.bfloat16)
    forward_sol, backward_sol = call(join_kernel, [whole] * 2, [mine, swap(sent, 1)])
    return forward_sol, backward_sol


def solution(mesh):
    return jax.shard_map(
        body,
        mesh=mesh,
        in_specs=(
            P(None, "rows", "rhs", None),
            P(None, "rows", None, None),
            P(None, "rows", "rhs", None, None),
            P(None, "rows", None),
        ),
        out_specs=(P(None, "rows", "rhs", None), P(None, "rows", "rhs", None)),
        check_vma=False,
    )
```

```python
import functools

import jax
import jax.numpy as jnp
from jax import lax
from jax.experimental import pallas as pl
from jax.experimental.pallas import tpu as pltpu
from jax.sharding import PartitionSpec as P

VMEM_SPEC = pl.BlockSpec(memory_space=pltpu.VMEM)
SMEM_SPEC = pl.BlockSpec(memory_space=pltpu.SMEM)
ANY_SPEC = pl.BlockSpec(memory_space=pl.ANY)
HBM_SPEC = pl.BlockSpec(memory_space=pltpu.HBM)
VMEM_GRANT = 8 * 1024 * 1024
PLANE = (6, 2, 4)


FIRST = 3
ROUND = 6
CROSS = (2,3)


def swap(value, mask):
    size = lax.axis_size("rows")
    return lax.ppermute(value, "rows", [(i, i ^ mask) for i in range(size)])


def times_transposed(left, right):
    return lax.dot_general(left, right, (((1,), (1,)), ((), ())), preferred_element_type=jnp.float32)


def times(left, right):
    return jnp.dot(left, right, preferred_element_type=jnp.float32)


def call(kernel, out_shape, operands, in_specs=None, scratch=(), flops=0):
    return pl.pallas_call(
        kernel,
        out_shape=out_shape,
        in_specs=[VMEM_SPEC] * len(operands) if in_specs is None else in_specs,
        out_specs=jax.tree.map(lambda _: VMEM_SPEC, out_shape),
        scratch_shapes=list(scratch),
        compiler_params=pltpu.CompilerParams(vmem_limit_bytes=VMEM_GRANT),
        cost_estimate=pl.CostEstimate(flops=flops, bytes_accessed=0, transcendentals=0),
    )(*operands)


def side(index):
    for bit in CROSS:
        index = index ^ ((index >> bit) & 1)
    return index & 1


def halves(width):
    mine = side(lax.axis_index("rows"))
    half = width // 2
    return (
        pl.ds(pl.multiple_of(mine * half, half), half),
        pl.ds(pl.multiple_of((1 - mine) * half, half), half),
    )


def first_kernel(rhs, diag, mine, sent, rhs_held, diag_held, arrived):
    here, there = halves(rhs.shape[2])
    loads = [
        pltpu.make_async_copy(rhs.at[0, 0], rhs_held, arrived.at[0]),
        pltpu.make_async_copy(diag.at[0, 0], diag_held, arrived.at[1]),
    ]
    for load in loads:
        load.start()
    for load in loads:
        load.wait()
    sent[...] = times_transposed(rhs_held[there], diag_held[...]).astype(sent.dtype)
    mine[...] = times_transposed(rhs_held[here], diag_held[...]).astype(mine.dtype)


def halve_kernel(after, rhs, rhs_mine, rhs_sent):
    here, there = halves(rhs.shape[2])
    for l in range(rhs.shape[0]):
        rhs_mine[l] = rhs[l, 0, here]
        rhs_sent[l] = rhs[l, 0, there]


def place_kernel(
    level, solve_levels, own_pattern, other_pattern, after, tiles0, tiles1, diag0, diag1, spread, diag, held, arrived
):
    me = lax.axis_index("rows")
    deep = spread.shape[1] // 8
    patterns, tiles = (own_pattern, other_pattern), (tiles0, tiles1)
    loads = []
    for i, inverse in enumerate((diag0, diag1)):
        for n, l in enumerate(solve_levels):
            loads.append(pltpu.make_async_copy(inverse.at[l, 0], diag.at[n, i], arrived.at[2 + 2 * n + i]))
    for load in loads:
        load.start()

    def clear():
        def clear_place(e, nothing):
            for i in range(2):
                spread[i, e] = jnp.zeros(spread.shape[2:], spread.dtype)
            return nothing

        lax.fori_loop(0, spread.shape[1], clear_place, 0)

    def place_of(i, k):
        away = jnp.bitwise_xor(patterns[i][level - 1, 0, k], me)
        flat = jnp.bitwise_and(away, 6)
        part = jnp.where(flat == PLANE[0], 1, jnp.where(flat == PLANE[1], 2, jnp.where(flat == PLANE[2], 3, 0)))
        return part * (2 * deep) + (away >> 3) * 2 + side(away)

    whole = [pltpu.make_async_copy(tiles[i].at[level - 1, 0], held.at[i], arrived.at[i]) for i in range(2)]

    def place_all():
        for load in whole:
            load.start()
        clear()
        for i in range(2):
            whole[i].wait()
            for k in range(held.shape[1]):
                spread[i, place_of(i, k)] = held[i, k]

    def place_few():
        clear()
        for i in range(2):
            for start in range(0, held.shape[1], ROUND):
                count = min(ROUND, held.shape[1] - start)
                for k in range(start, start + count):
                    tile = tiles[i].at[level - 1, 0, k]
                    pltpu.make_async_copy(tile, spread.at[i, place_of(i, k)], arrived.at[i]).start()
                some = tiles[i].at[level - 1, 0, pl.ds(start, count)]
                pltpu.make_async_copy(some, spread.at[i, pl.ds(0, count)], arrived.at[i]).wait()

    if level == 1:
        group = side(me)
        pl.when(group == 0)(place_all)
        pl.when(group == 1)(place_few)
    else:
        place_all()
    for load in loads:
        load.wait()


def meet(part, spread, i, j):
    deep = part.shape[0]
    total = None
    for z in range(deep):
        for s in range(2):
            term = times_transposed(part[z, s], spread[i, j * 2 * deep + 2 * z + s])
            total = term if total is None else total + term
    return total


def more_kernel(j, spread, part, *refs):
    terms = [meet(part, spread, i, j) for i in range(2)]
    for i in range(2):
        refs[-1][i] = refs[0][i] + terms[i] if len(refs) > 1 else terms[i]


def finish(spread, late, partial, rhs, diag):
    terms = [None, None]
    for j, part in late:
        for i in range(2):
            term = meet(part, spread, i, j)
            terms[i] = term if terms[i] is None else terms[i] + term
    residuals = []
    for i in range(2):
        coupled = terms[i] if partial is None else partial[i] + terms[i]
        residuals.append((rhs[i].astype(jnp.float32) - coupled).astype(jnp.bfloat16))
    return [times_transposed(residuals[i], diag[i]).astype(jnp.bfloat16) for i in range(2)]


def push(solved, spread, j, out):
    deep = out.shape[0]
    for z in range(deep):
        for s in range(2):
            e = j * 2 * deep + 2 * z + s
            total = times(solved[0], spread[0, e]) + times(solved[1], spread[1, e])
            out[z, s] = total.astype(out.dtype)


def forward_kernel(level, first, spread, r0, r1, diag, *refs):
    late, partial, out = list(enumerate(refs[: 4 - first], first)), refs[4 - first] if first else None, refs[-1]
    out[0], out[1] = finish(spread, late, partial, (r0[level], r1[level]), diag)


def turn_kernel(level, first, spread, r0, r1, diag, *refs):
    late, partial, (out, back, o1, o2, o3) = list(enumerate(refs[: 4 - first], first)), refs[4 - first], refs[-5:]
    solved = finish(spread, late, partial, (r0[level], r1[level]), diag)
    out[0], out[1] = solved
    down = [times(solved[i], diag[i]).astype(jnp.bfloat16) for i in range(2)]
    back[0], back[1] = down
    for j, part in enumerate((o1, o2, o3)):
        push(down, spread, j + 1, part)


def keep_kernel(spread, back, keep):
    push((back[0], back[1]), spread, 0, keep)


def reduce_kernel(keep, a, b, c, own, *outs):
    for z in range(keep.shape[0]):
        terms = [part[z].astype(jnp.float32) for part in (a, b, c)]
        value = keep[z] + ((terms[0] + terms[1]) + terms[2])
        if z == 0:
            own[...] = value
        else:
            outs[z - 1][...] = value.astype(jnp.bfloat16)


def backward_step(own, arrived, known, diag):
    pushed = own[...]
    for part in arrived:
        pushed = pushed + part[...].astype(jnp.float32)
    residual = (known[...].astype(jnp.float32) - pushed).astype(jnp.bfloat16)
    return [times(residual[i], diag[i]).astype(jnp.bfloat16) for i in range(2)]


def backward_kernel(spread, own, known, diag, *refs):
    arrived, (back, o1, o2, o3) = refs[:-4], refs[-4:]
    down = backward_step(own, arrived, known, diag)
    back[0], back[1] = down
    for j, part in enumerate((o1, o2, o3)):
        push(down, spread, j + 1, part)


def last_kernel(own, known, diag, *refs):
    arrived, (mine, sent) = refs[:-2], refs[-2:]
    mine[...], sent[...] = backward_step(own, arrived, known, diag)


def split_kernel(*refs):
    blocks, (mine, sent) = refs[:-2], refs[-2:]
    for l, block in enumerate(blocks):
        mine[l] = block[0]
        sent[l] = block[1]


def join_kernel(*refs):
    pairs, out = refs[:-1], refs[-1]
    here, there = halves(out.shape[2])
    l = 0
    for mine, other in zip(pairs[0::2], pairs[1::2]):
        for m in range(mine.shape[0]):
            out[l, 0, here] = mine[m]
            out[l, 0, there] = other[m]
            l += 1


def body(rhs_block, diag_inv, off_tiles, pattern):
    levels, _, width, size = rhs_block.shape
    devices = lax.axis_size("rows")
    half = width // 2
    line = [8 * j + side(8 * j) for j in range(1, devices // 8)]
    plane = [m + side(m) for m in PLANE]
    deep = len(line) + 1
    if lax.axis_size("rhs") > 1:
        off_tiles = lax.all_gather(off_tiles, "rhs", axis=2, tiled=True)

    def shape(*dims, dtype=jnp.bfloat16):
        return jax.ShapeDtypeStruct(dims + (half, size), dtype)

    def in_hbm(value):
        return pltpu.with_memory_space_constraint(value, pltpu.HBM)

    own_tiles, diag_own = in_hbm(off_tiles), in_hbm(diag_inv)
    mine, sent = call(
        first_kernel,
        [shape()] * 2,
        [in_hbm(rhs_block), diag_own],
        [HBM_SPEC] * 2,
        scratch=[
            pltpu.VMEM((width, size), jnp.bfloat16),
            pltpu.VMEM((size, size), jnp.bfloat16),
            pltpu.SemaphoreType.DMA((2,)),
        ],
    )
    other_pattern = swap(pattern, 1)
    other = swap(sent, 1)
    rhs_own, rhs_sent = call(halve_kernel, [shape(levels)] * 2, [sent, rhs_block])
    rhs_sent, diag_sent, tiles_sent, other, other_pattern = lax.optimization_barrier(
        (rhs_sent, diag_inv, off_tiles, other, other_pattern)
    )
    forward = [jnp.stack([mine, other])]
    rhs_other, diag_other, other_tiles = swap(rhs_sent, 1), swap(diag_sent, 1), swap(tiles_sent, 1)
    work = 2 * 2 * devices // 4 * half * size * size
    diag = [None] * levels

    def along(block):
        return [block] + [swap(block, m) for m in line]

    def placed(level, block):
        solve_levels = (1, 0) if level == 1 else (level,)
        spread, inverses = call(
            functools.partial(place_kernel, level, solve_levels),
            [
                pltpu.VMEM((2, devices, size, size), jnp.bfloat16),
                pltpu.VMEM((len(solve_levels), 2, size, size), jnp.bfloat16),
            ],
            [in_hbm(pattern), other_pattern, block, own_tiles, other_tiles, diag_own, diag_other],
            [SMEM_SPEC] * 2 + [VMEM_SPEC] + [HBM_SPEC, ANY_SPEC] * 2,
            scratch=[
                pltpu.VMEM((2,) + off_tiles.shape[2:], jnp.bfloat16),
                pltpu.SemaphoreType.DMA((2 + 2 * len(solve_levels),)),
            ],
            flops=2 * work,
        )
        for n, l in enumerate(solve_levels):
            diag[l] = inverses[n]
        return spread

    def met(level, arrived, spread, first):
        parts = [jnp.stack(arrived)]
        parts += [swap(parts[0], m) for m in plane]
        partial = []
        for j in range(first):
            kernel = functools.partial(more_kernel, j)
            partial = [call(kernel, shape(2, dtype=jnp.float32), [spread, parts[j]] + partial, flops=work)]
        return [spread, rhs_own, rhs_other, diag[level]] + parts[first:] + partial

    def scattered(spread, back, outs):
        keep = call(keep_kernel, shape(deep, 2, dtype=jnp.float32), [spread, back], flops=work)
        arrived = [swap(out, m) for out, m in zip(outs, plane)]
        summed = call(reduce_kernel, [shape(2, dtype=jnp.float32)] + [shape(2)] * (deep - 1), [keep] + arrived)
        return summed[0], [swap(part, m) for part, m in zip(summed[1:], line)]

    arrived = along(forward[0])
    spreads = [placed(1, forward[0])]
    for l in range(1, levels - 1):
        first = FIRST
        operands = met(l, arrived, spreads[-1], first)
        forward.append(call(functools.partial(forward_kernel, l, first), shape(2), operands, flops=work))
        arrived = along(forward[l])
        spread = placed(l + 1, forward[l])
        *arrived, spread = lax.optimization_barrier((*arrived, spread))
        spreads.append(spread)
    l = levels - 1
    operands = met(l, arrived, spreads[-1], FIRST)
    top, back, *outs = call(
        functools.partial(turn_kernel, l, FIRST), [shape(2)] * 2 + [shape(deep, 2)] * 3, operands, flops=4 * work
    )
    forward.append(top)
    backward = [back]
    for l in range(levels - 2, 0, -1):
        own, arrived = scattered(spreads[l], back, outs)
        back, *outs = call(
            backward_kernel,
            [shape(2)] + [shape(deep, 2)] * 3,
            [spreads[l - 1], own, forward[l], diag[l]] + arrived,
            flops=3 * work,
        )
        backward.insert(0, back)
    own, arrived = scattered(spreads[0], back, outs)
    last, last_sent = call(last_kernel, [shape()] * 2, [own, forward[0], diag[0]] + arrived)

    whole = jax.ShapeDtypeStruct((levels, 1, width, size), jnp.bfloat16)
    mine, sent = call(split_kernel, [shape(levels)] * 2, forward)
    forward_sol = call(join_kernel, whole, [mine, swap(sent, 1)])
    mine, sent = call(split_kernel, [shape(levels - 1)] * 2, backward)
    backward_sol = call(join_kernel, whole, [last[None], swap(last_sent, 1)[None], mine, swap(sent, 1)])
    return forward_sol, backward_sol


def solution(mesh):
    return jax.shard_map(
        body,
        mesh=mesh,
        in_specs=(
            P(None, "rows", "rhs", None),
            P(None, "rows", None, None),
            P(None, "rows", "rhs", None, None),
            P(None, "rows", None),
        ),
        out_specs=(P(None, "rows", "rhs", None), P(None, "rows", "rhs", None)),
        check_vma=False,
    )
```

```python
import functools

import jax
import jax.numpy as jnp
from jax import lax
from jax.experimental import pallas as pl
from jax.experimental.pallas import tpu as pltpu
from jax.sharding import PartitionSpec as P

VMEM_SPEC = pl.BlockSpec(memory_space=pltpu.VMEM)
SMEM_SPEC = pl.BlockSpec(memory_space=pltpu.SMEM)
ANY_SPEC = pl.BlockSpec(memory_space=pl.ANY)
HBM_SPEC = pl.BlockSpec(memory_space=pltpu.HBM)
VMEM_GRANT = 8 * 1024 * 1024
PLANE = (6, 2, 4)


FIRST = 3
ROUND = 6
CROSS = (2,3)


def swap(value, mask):
    size = lax.axis_size("rows")
    return lax.ppermute(value, "rows", [(i, i ^ mask) for i in range(size)])


def times_transposed(left, right):
    return lax.dot_general(left, right, (((1,), (1,)), ((), ())), preferred_element_type=jnp.float32)


def times(left, right):
    return jnp.dot(left, right, preferred_element_type=jnp.float32)


def call(kernel, out_shape, operands, in_specs=None, scratch=(), flops=0):
    return pl.pallas_call(
        kernel,
        out_shape=out_shape,
        in_specs=[VMEM_SPEC] * len(operands) if in_specs is None else in_specs,
        out_specs=jax.tree.map(lambda _: VMEM_SPEC, out_shape),
        scratch_shapes=list(scratch),
        compiler_params=pltpu.CompilerParams(vmem_limit_bytes=VMEM_GRANT),
        cost_estimate=pl.CostEstimate(flops=flops, bytes_accessed=0, transcendentals=0),
    )(*operands)


def side(index):
    for bit in CROSS:
        index = index ^ ((index >> bit) & 1)
    return index & 1


def halves(width):
    mine = side(lax.axis_index("rows"))
    half = width // 2
    return (
        pl.ds(pl.multiple_of(mine * half, half), half),
        pl.ds(pl.multiple_of((1 - mine) * half, half), half),
    )


def first_kernel(rhs, diag, mine, sent, rhs_held, diag_held, arrived):
    here, there = halves(rhs.shape[2])
    loads = [
        pltpu.make_async_copy(rhs.at[0, 0], rhs_held, arrived.at[0]),
        pltpu.make_async_copy(diag.at[0, 0], diag_held, arrived.at[1]),
    ]
    for load in loads:
        load.start()
    for load in loads:
        load.wait()
    sent[...] = times_transposed(rhs_held[there], diag_held[...]).astype(sent.dtype)
    mine[...] = times_transposed(rhs_held[here], diag_held[...]).astype(mine.dtype)


def halve_kernel(after, rhs, rhs_mine, rhs_sent):
    here, there = halves(rhs.shape[2])
    for l in range(rhs.shape[0]):
        rhs_mine[l] = rhs[l, 0, here]
        rhs_sent[l] = rhs[l, 0, there]


def place_kernel(
    level, solve_levels, own_pattern, other_pattern, after, tiles0, tiles1, diag0, diag1, spread, diag, held, arrived
):
    me = lax.axis_index("rows")
    deep = spread.shape[1] // 8
    patterns, tiles = (own_pattern, other_pattern), (tiles0, tiles1)
    loads = []
    for i, inverse in enumerate((diag0, diag1)):
        for n, l in enumerate(solve_levels):
            loads.append(pltpu.make_async_copy(inverse.at[l, 0], diag.at[n, i], arrived.at[2 + 2 * n + i]))
    for load in loads:
        load.start()

    def clear():
        def clear_place(e, nothing):
            for i in range(2):
                spread[i, e] = jnp.zeros(spread.shape[2:], spread.dtype)
            return nothing

        lax.fori_loop(0, spread.shape[1], clear_place, 0)

    def place_of(i, k):
        away = jnp.bitwise_xor(patterns[i][level - 1, 0, k], me)
        flat = jnp.bitwise_and(away, 6)
        part = jnp.where(flat == PLANE[0], 1, jnp.where(flat == PLANE[1], 2, jnp.where(flat == PLANE[2], 3, 0)))
        return part * (2 * deep) + (away >> 3) * 2 + side(away)

    whole = [pltpu.make_async_copy(tiles[i].at[level - 1, 0], held.at[i], arrived.at[i]) for i in range(2)]

    def place_all():
        for load in whole:
            load.start()
        clear()
        for i in range(2):
            whole[i].wait()
            for k in range(held.shape[1]):
                spread[i, place_of(i, k)] = held[i, k]

    def place_few():
        clear()
        for i in range(2):
            for start in range(0, held.shape[1], ROUND):
                count = min(ROUND, held.shape[1] - start)
                for k in range(start, start + count):
                    tile = tiles[i].at[level - 1, 0, k]
                    pltpu.make_async_copy(tile, spread.at[i, place_of(i, k)], arrived.at[i]).start()
                some = tiles[i].at[level - 1, 0, pl.ds(start, count)]
                pltpu.make_async_copy(some, spread.at[i, pl.ds(0, count)], arrived.at[i]).wait()

    if level == 1:
        group = side(me)
        pl.when(group == 0)(place_all)
        pl.when(group == 1)(place_few)
    else:
        place_all()
    for load in loads:
        load.wait()


def meet(part, spread, i, j):
    deep = part.shape[0]
    total = None
    for z in range(deep):
        for s in range(2):
            term = times_transposed(part[z, s], spread[i, j * 2 * deep + 2 * z + s])
            total = term if total is None else total + term
    return total


def more_kernel(j, spread, part, *refs):
    terms = [meet(part, spread, i, j) for i in range(2)]
    for i in range(2):
        refs[-1][i] = refs[0][i] + terms[i] if len(refs) > 1 else terms[i]


def early_kernel(spread, *refs):
    parts, out = refs[:-1], refs[-1]
    totals = []
    for i in range(2):
        terms = [meet(part, spread, i, j) for j, part in enumerate(parts)]
        totals.append(sum(terms[1:], terms[0]))
    for i in range(2):
        out[i] = totals[i]


def finish(spread, late, partial, rhs, diag):
    terms = [None, None]
    for j, part in late:
        for i in range(2):
            term = meet(part, spread, i, j)
            terms[i] = term if terms[i] is None else terms[i] + term
    residuals = []
    for i in range(2):
        coupled = terms[i] if partial is None else partial[i] + terms[i]
        residuals.append((rhs[i].astype(jnp.float32) - coupled).astype(jnp.bfloat16))
    return [times_transposed(residuals[i], diag[i]).astype(jnp.bfloat16) for i in range(2)]


def push(solved, spread, j, out):
    deep = out.shape[0]
    for z in range(deep):
        for s in range(2):
            e = j * 2 * deep + 2 * z + s
            total = times(solved[0], spread[0, e]) + times(solved[1], spread[1, e])
            out[z, s] = total.astype(out.dtype)


def forward_kernel(level, first, spread, r0, r1, diag, *refs):
    late, partial, out = list(enumerate(refs[: 4 - first], first)), refs[4 - first] if first else None, refs[-1]
    out[0], out[1] = finish(spread, late, partial, (r0[level], r1[level]), diag)


def turn_kernel(level, first, spread, r0, r1, diag, *refs):
    late, partial, (out, back, o1, o2, o3) = list(enumerate(refs[: 4 - first], first)), refs[4 - first], refs[-5:]
    solved = finish(spread, late, partial, (r0[level], r1[level]), diag)
    out[0], out[1] = solved
    down = [times(solved[i], diag[i]).astype(jnp.bfloat16) for i in range(2)]
    back[0], back[1] = down
    for j, part in enumerate((o1, o2, o3)):
        push(down, spread, j + 1, part)


def keep_kernel(spread, back, keep):
    push((back[0], back[1]), spread, 0, keep)


def reduce_kernel(keep, a, b, c, own, *outs):
    for z in range(keep.shape[0]):
        terms = [part[z].astype(jnp.float32) for part in (a, b, c)]
        value = keep[z] + ((terms[0] + terms[1]) + terms[2])
        if z == 0:
            own[...] = value
        else:
            outs[z - 1][...] = value.astype(jnp.bfloat16)


def backward_step(own, arrived, known, diag):
    pushed = own[...]
    for part in arrived:
        pushed = pushed + part[...].astype(jnp.float32)
    residual = (known[...].astype(jnp.float32) - pushed).astype(jnp.bfloat16)
    return [times(residual[i], diag[i]).astype(jnp.bfloat16) for i in range(2)]


def backward_kernel(spread, own, known, diag, *refs):
    arrived, (back, o1, o2, o3) = refs[:-4], refs[-4:]
    down = backward_step(own, arrived, known, diag)
    back[0], back[1] = down
    for j, part in enumerate((o1, o2, o3)):
        push(down, spread, j + 1, part)


def last_kernel(own, known, diag, *refs):
    arrived, (mine, sent) = refs[:-2], refs[-2:]
    mine[...], sent[...] = backward_step(own, arrived, known, diag)


def split_kernel(*refs):
    blocks, (mine, sent) = refs[:-2], refs[-2:]
    for l, block in enumerate(blocks):
        mine[l] = block[0]
        sent[l] = block[1]


def join_kernel(*refs):
    pairs, out = refs[:-1], refs[-1]
    here, there = halves(out.shape[2])
    l = 0
    for mine, other in zip(pairs[0::2], pairs[1::2]):
        for m in range(mine.shape[0]):
            out[l, 0, here] = mine[m]
            out[l, 0, there] = other[m]
            l += 1


def body(rhs_block, diag_inv, off_tiles, pattern):
    levels, _, width, size = rhs_block.shape
    devices = lax.axis_size("rows")
    half = width // 2
    line = [8 * j + side(8 * j) for j in range(1, devices // 8)]
    plane = [m + side(m) for m in PLANE]
    deep = len(line) + 1
    if lax.axis_size("rhs") > 1:
        off_tiles = lax.all_gather(off_tiles, "rhs", axis=2, tiled=True)

    def shape(*dims, dtype=jnp.bfloat16):
        return jax.ShapeDtypeStruct(dims + (half, size), dtype)

    def in_hbm(value):
        return pltpu.with_memory_space_constraint(value, pltpu.HBM)

    own_tiles, diag_own = in_hbm(off_tiles), in_hbm(diag_inv)
    mine, sent = call(
        first_kernel,
        [shape()] * 2,
        [in_hbm(rhs_block), diag_own],
        [HBM_SPEC] * 2,
        scratch=[
            pltpu.VMEM((width, size), jnp.bfloat16),
            pltpu.VMEM((size, size), jnp.bfloat16),
            pltpu.SemaphoreType.DMA((2,)),
        ],
    )
    other_pattern = swap(pattern, 1)
    other = swap(sent, 1)
    rhs_own, rhs_sent = call(halve_kernel, [shape(levels)] * 2, [sent, rhs_block])
    rhs_sent, diag_sent, tiles_sent, other, other_pattern = lax.optimization_barrier(
        (rhs_sent, diag_inv, off_tiles, other, other_pattern)
    )
    forward = [jnp.stack([mine, other])]
    rhs_other, diag_other, other_tiles = swap(rhs_sent, 1), swap(diag_sent, 1), swap(tiles_sent, 1)
    work = 2 * 2 * devices // 4 * half * size * size
    diag = [None] * levels

    def along(block):
        return [block] + [swap(block, m) for m in line]

    def placed(level, block):
        solve_levels = (1, 0) if level == 1 else (level,)
        spread, inverses = call(
            functools.partial(place_kernel, level, solve_levels),
            [
                pltpu.VMEM((2, devices, size, size), jnp.bfloat16),
                pltpu.VMEM((len(solve_levels), 2, size, size), jnp.bfloat16),
            ],
            [in_hbm(pattern), other_pattern, block, own_tiles, other_tiles, diag_own, diag_other],
            [SMEM_SPEC] * 2 + [VMEM_SPEC] + [HBM_SPEC, ANY_SPEC] * 2,
            scratch=[
                pltpu.VMEM((2,) + off_tiles.shape[2:], jnp.bfloat16),
                pltpu.SemaphoreType.DMA((2 + 2 * len(solve_levels),)),
            ],
            flops=2 * work,
        )
        for n, l in enumerate(solve_levels):
            diag[l] = inverses[n]
        return spread

    def met(level, arrived, spread, first):
        parts = [jnp.stack(arrived)]
        parts += [swap(parts[0], m) for m in plane]
        partial = []
        if level == 1:
            partial = [call(early_kernel, shape(2, dtype=jnp.float32), [spread] + parts[:first], flops=first * work)]
        for j in range(first if level > 1 else 0):
            kernel = functools.partial(more_kernel, j)
            partial = [call(kernel, shape(2, dtype=jnp.float32), [spread, parts[j]] + partial, flops=work)]
        return [spread, rhs_own, rhs_other, diag[level]] + parts[first:] + partial

    def scattered(spread, back, outs):
        keep = call(keep_kernel, shape(deep, 2, dtype=jnp.float32), [spread, back], flops=work)
        arrived = [swap(out, m) for out, m in zip(outs, plane)]
        summed = call(reduce_kernel, [shape(2, dtype=jnp.float32)] + [shape(2)] * (deep - 1), [keep] + arrived)
        return summed[0], [swap(part, m) for part, m in zip(summed[1:], line)]

    arrived = along(forward[0])
    spreads = [placed(1, forward[0])]
    for l in range(1, levels - 1):
        first = FIRST
        operands = met(l, arrived, spreads[-1], first)
        forward.append(call(functools.partial(forward_kernel, l, first), shape(2), operands, flops=work))
        arrived = along(forward[l])
        spread = placed(l + 1, forward[l])
        *arrived, spread = lax.optimization_barrier((*arrived, spread))
        spreads.append(spread)
    l = levels - 1
    operands = met(l, arrived, spreads[-1], FIRST)
    top, back, *outs = call(
        functools.partial(turn_kernel, l, FIRST), [shape(2)] * 2 + [shape(deep, 2)] * 3, operands, flops=4 * work
    )
    forward.append(top)
    backward = [back]
    for l in range(levels - 2, 0, -1):
        own, arrived = scattered(spreads[l], back, outs)
        back, *outs = call(
            backward_kernel,
            [shape(2)] + [shape(deep, 2)] * 3,
            [spreads[l - 1], own, forward[l], diag[l]] + arrived,
            flops=3 * work,
        )
        backward.insert(0, back)
    own, arrived = scattered(spreads[0], back, outs)
    last, last_sent = call(last_kernel, [shape()] * 2, [own, forward[0], diag[0]] + arrived)

    whole = jax.ShapeDtypeStruct((levels, 1, width, size), jnp.bfloat16)
    mine, sent = call(split_kernel, [shape(levels)] * 2, forward)
    forward_sol = call(join_kernel, whole, [mine, swap(sent, 1)])
    mine, sent = call(split_kernel, [shape(levels - 1)] * 2, backward)
    backward_sol = call(join_kernel, whole, [last[None], swap(last_sent, 1)[None], mine, swap(sent, 1)])
    return forward_sol, backward_sol


def solution(mesh):
    return jax.shard_map(
        body,
        mesh=mesh,
        in_specs=(
            P(None, "rows", "rhs", None),
            P(None, "rows", None, None),
            P(None, "rows", "rhs", None, None),
            P(None, "rows", None),
        ),
        out_specs=(P(None, "rows", "rhs", None), P(None, "rows", "rhs", None)),
        check_vma=False,
    )
```
